32 devices in a mesh: blk: 8 (over y, x, core), sub: 4 (over z).
Axes of the slice: x: 2, y: 2, z: 4, core: 2. Of those that a mesh axis runs over, the one named last changes fastest.
Arguments:
- tracer: float32 [80, 2, 64, 1024], P(None, None, 'sub', 'blk'), may hold values from -6 to 6
- velocity: float32 [2, 80, 64, 1024], P(None, None, 'sub', 'blk'), may hold values from -0.3 to 0.3
- kappa: float32 [79, 64, 1024], P(None, 'sub', 'blk'), may hold values from 0.02 to 200
- kmt: int32 [64, 1024], P('sub', 'blk'), may hold values from 1 to 80
- land_mask: int32 [64, 1024], P('sub', 'blk'), may hold values 0 or 1
- atm_flux: float32 [2, 196608], P(None, ('blk', 'sub')), may hold values from -6 to 6
- remap_weight: bfloat16 [2048, 128, 128], P(('blk', 'sub')), may hold values from -0.5 to 0.5
- remap_dest: int32 [2048, 1], P(('blk', 'sub')), may hold values from 0 to 31; in each aligned block of 64 rows (0 to 63, 64 to 127, ...) at most 4 rows name the same one
- remap_src_block: int32 [2048], P(('blk', 'sub')), may hold values from 0 to 47
- remap_dst_block: int32 [2048], P(('blk', 'sub')), may hold values from 0 to 15
Outputs:
- tracer_out: float32 [80, 2, 64, 1024], P(None, None, 'sub', 'blk')
- atmosphere_surface_tracer: float32 [2, 196608], P(None, ('blk', 'sub'))
The draws below stay inside these ranges and needn't reach their ends.
Inputs may be any that keep to these rules, and one draw needn't show every extreme that they name: `remap_dest`: among the 64 tiles of one device, no destination device is named more than 4 times, a bound that some block reaches.
All inputs are finite; a program needn't handle non-finite values. No bound on the sum of `land_mask` on one device may be relied on, other than what follows from the above.
Results may differ from the reference program's by a relative error of at most 0.0003.
Values sent between devices are 32-bit elements; how exact they have to be, the bound alone decides.
A program may use at most 192 MiB of HBM per device.

```python
import math
import jax
import jax.numpy as jnp
import numpy as np
from jax import lax

L = 80
TRACER_COUNT = 2
NXC = 128
NYC = 16
ABLK = 48
KT = 64
NSTEP = 4
CAP = 4
NY = 64
NX = 1024
ATMOS_COLUMNS = 196608
NTILE = 2048
N_BLK = 8
N_SUB = 4
DEVICES = 32


def deep_select(key):
    return jax.random.randint(jax.random.fold_in(key, 71), (NY, NX), 0, 4) == 0


def draw_kmt(key, part):
    deep_mask = deep_select(key)
    shallow_levels = jax.random.randint(jax.random.fold_in(key, 72), (NY, NX), 1, L + 1)
    return jnp.where(deep_mask, L, shallow_levels).astype(jnp.int32)


def draw_kappa(key, part):
    deep_mask = deep_select(key)
    base_values = jnp.exp(jax.random.uniform(jax.random.fold_in(key, 73), (L - 1, NY, NX), jnp.float32, math.log(0.02), math.log(20.0)))
    level_factor = jax.random.uniform(jax.random.fold_in(key, 74), (L - 1, NY, NX), jnp.float32, 0.8, 1.25)
    column_value = jnp.exp(jax.random.uniform(jax.random.fold_in(key, 75), (1, NY, NX), jnp.float32, math.log(25.0), math.log(160.0)))
    deep_values = column_value * level_factor
    return jnp.where(deep_mask[None], deep_values, base_values).astype(jnp.float32)


def draw_velocity(key, part):
    sign_key = jax.random.fold_in(key, 81)
    size_key = jax.random.fold_in(key, 82)
    block_rows = NY // 4 + 1
    block_cols = NX // 32 + 1
    sign_draw = jax.random.randint(sign_key, (2, L, block_rows, block_cols), 0, 2)
    sign_field = jnp.where(sign_draw == 1, 1.0, -1.0).astype(jnp.float32)
    sign_field = jnp.repeat(jnp.repeat(sign_field, 4, axis=2), 32, axis=3)[:, :, :NY, :NX]
    magnitude = jax.random.uniform(size_key, (2, L, NY, NX), jnp.float32, 0.05, 0.3)
    return (sign_field * magnitude).astype(jnp.float32)


def place_ends(array, key, smallest, high):
    index_at = [jax.random.randint(jax.random.fold_in(key, axis), (), 0, length) for axis, length in enumerate(array.shape)]
    main_axis = array.shape.index(max(array.shape))
    beside = index_at[:main_axis] + [(index_at[main_axis] + 1) % array.shape[main_axis]] + index_at[main_axis + 1:]
    return array.at[tuple(index_at)].set(smallest).at[tuple(beside)].set(high)


def levels(rng, dims, split, low, high):
    loudness = 1.0
    for dim, parts in split:
        draws = jax.random.uniform(jax.random.fold_in(jax.random.fold_in(rng, 6), dim), (parts,), jnp.float32, low / len(split), high / len(split))
        loudness = loudness * jnp.repeat(jnp.exp(draws), dims[dim] // parts).reshape((-1,) + (1,) * (len(dims) - 1 - dim))
    return loudness


def assign_block(key, own, number, rows, count, top, limit, slope):
    sequence = jax.random.permutation(key, count)
    packed, ordinary = load_shares(count, rows * top, limit, slope, True), load_shares(count, rows * top, limit, slope, False)
    places = jnp.arange(count)

    def named(tallies, rotation):
        used = int((tallies > 0).sum())
        fixed = max(1, used // 4)
        moved = fixed + (places - fixed + rotation * (used - fixed)) % max(1, count - fixed)
        return jnp.zeros((count,), jnp.int32).at[sequence[jnp.where(places < fixed, places, moved)]].set(jnp.asarray(tallies, jnp.int32))

    tallies = jnp.where(number % 4 == 0, named(packed, number // 4), named(ordinary, number - number // 4 - 1))
    mixed = jax.random.permutation(jax.random.fold_in(own, 3), count)
    donor, receiver = mixed[0:count // 2 * 2:2], mixed[1:count // 2 * 2:2]
    margin = jnp.minimum(tallies[donor] - 1, limit - tallies[receiver]) // 2
    margin = jnp.where((donor == sequence[0]) | (receiver == sequence[0]) | (tallies[receiver] == 0), 0, jnp.maximum(margin, 0))
    moved = jax.random.randint(jax.random.fold_in(own, 4), (count // 2,), 0, 1 << 20) % (margin + 1)
    tallies = tallies.at[donor].add(-moved).at[receiver].add(moved)
    members = jnp.searchsorted(jnp.cumsum(tallies), jnp.arange(rows * top), side="right").astype(jnp.int32)
    listing = members.reshape(top, rows).T
    listing = listing[jax.random.permutation(jax.random.fold_in(own, 1), rows)]
    rotation = jax.random.randint(jax.random.fold_in(own, 2), (rows, 1), 0, top)
    return jnp.take_along_axis(listing, (jnp.arange(top)[None, :] + rotation) % top, axis=1)


def load_shares(number_of, total, reach, slope, full):
    weights = [(1 << 20) // math.isqrt(grade ** slope) + 1 for grade in range(1, number_of + 1)]
    largest = reach if full else min(reach, max(-(-total // number_of), total * weights[0] // sum(weights)))
    least = 1 if total - largest >= number_of - 1 else 0
    counts, rest = [largest] + [least] * (number_of - 1), total - largest - least * (number_of - 1)
    while rest > 0:
        free = [i for i in range(1, number_of) if counts[i] < largest] or [i for i in range(1, number_of) if counts[i] < reach]
        whole, left = sum([weights[i] for i in free]), rest
        for i in free:
            addition = min(reach - counts[i], max(1, left * weights[i] // whole), rest)
            counts[i] = counts[i] + addition
            rest = rest - addition
    return np.array(counts)


def scatter_about(stream_key, dims, spread, most, cuts=(), held_as=jnp.bfloat16):
    drawn = spread * jax.random.normal(stream_key, dims, jnp.float32)
    if cuts:
        drawn = drawn * levels(stream_key, dims, cuts, -0.22, 0.18)
    return jnp.clip(drawn, -most, most).astype(held_as)


def setup_inputs(seed: int = 0) -> dict:
    splits = jax.random.split(jax.random.key(seed), 11)
    tracer = scatter_about(splits[0], (L, TRACER_COUNT, NY, NX), 1.0, 6.0, ((2, 4), (3, 8)), jnp.float32)
    velocity = draw_velocity(jax.random.fold_in(splits[10], 71), 0)
    kappa = draw_kappa(jax.random.fold_in(splits[10], 71), 0)
    kmt = draw_kmt(jax.random.fold_in(splits[10], 71), 0)
    land_mask = place_ends((jax.random.randint(splits[4], (NY, NX), 0, 10) < 7).astype(jnp.int32), jax.random.fold_in(splits[4], 1), 0, 1)
    atm_flux = scatter_about(splits[5], (TRACER_COUNT, ATMOS_COLUMNS), 1.0, 6.0, ((1, 32),), jnp.float32)
    remap_weight = scatter_about(splits[6], (NTILE, NXC, NXC), NXC ** -0.5, 0.5, ((0, 32),))
    remap_dest_keys = jax.random.split(jax.random.fold_in(splits[7], 1), NTILE // KT)
    remap_dest_turns = jax.random.permutation(jax.random.fold_in(splits[7], 3), NTILE // KT)
    remap_dest = jax.vmap(lambda own, number: assign_block(jax.random.fold_in(splits[7], 2), own, number, KT, DEVICES, 1, CAP, 2))(remap_dest_keys, remap_dest_turns).reshape((NTILE, 1))
    remap_src_block = place_ends(jax.random.randint(splits[8], (NTILE,), 0, ABLK), jax.random.fold_in(splits[8], 1), 0, ABLK - 1).astype(jnp.int32)
    remap_dst_block = place_ends(jax.random.randint(splits[9], (NTILE,), 0, NYC), jax.random.fold_in(splits[9], 1), 0, NYC - 1).astype(jnp.int32)
    return {"tracer": tracer, "velocity": velocity, "kappa": kappa, "kmt": kmt, "land_mask": land_mask, "atm_flux": atm_flux, "remap_weight": remap_weight, "remap_dest": remap_dest, "remap_src_block": remap_src_block, "remap_dst_block": remap_dst_block}


FORCE = 0.25
HIGH = lax.Precision.HIGHEST


def column_solve(rhs, couple):
    zero = jnp.zeros_like(couple[:1])
    above = jnp.concatenate([zero, couple], axis=0)
    below = jnp.concatenate([couple, zero], axis=0)
    diag = 1.0 + above + below

    def forward(carry, items):
        cprev, dprev = carry
        a_up, a_down, centre, value = items
        denom = centre + a_up * cprev
        cnow = -a_down / denom
        dnow = (value + a_up[None] * dprev) / denom[None]
        return (cnow, dnow), (cnow, dnow)

    start = (jnp.zeros(couple.shape[1:], jnp.float32), jnp.zeros(rhs.shape[1:], jnp.float32))
    _, (cfac, dfac) = lax.scan(forward, start, (above, below, diag, rhs))

    def backward(xnext, items):
        cnow, dnow = items
        xnow = dnow - cnow[None] * xnext
        return xnow, xnow

    _, solved = lax.scan(backward, jnp.zeros(rhs.shape[1:], jnp.float32), (cfac, dfac), reverse=True)
    return solved


def reference(tracer, velocity, kappa, kmt, land_mask, atm_flux, remap_weight, remap_dest, remap_src_block, remap_dst_block):
    land = jnp.where(land_mask > 0, 1.0, 0.0).astype(jnp.float32)
    level = lax.broadcasted_iota(jnp.int32, (L, NY, NX), 0)
    wet = jnp.where(level < kmt[None], land[None], 0.0).astype(jnp.float32)
    couple = kappa * jnp.where(level[1:] < kmt[None], land[None], 0.0).astype(jnp.float32)

    tile_dev = jnp.arange(NTILE, dtype=jnp.int32) // KT
    gsrc = (tile_dev * ABLK + remap_src_block).astype(jnp.int32)
    dest = remap_dest[:, 0]
    grow = ((dest % N_SUB) * NYC + remap_dst_block).astype(jnp.int32)
    gcol = (dest // N_SUB).astype(jnp.int32)
    atm = atm_flux.reshape(TRACER_COUNT, DEVICES * ABLK, NXC)
    blocks = jnp.transpose(atm[:, gsrc], (1, 0, 2))
    weights = remap_weight.reshape(DEVICES, KT, NXC, NXC)

    def forward_map(item):
        rows_in, tiles = item
        return jnp.einsum("tfa,tab->tfb", rows_in, tiles.astype(jnp.float32), precision=HIGH)

    contrib = lax.map(forward_map, (blocks.reshape(DEVICES, KT, TRACER_COUNT, NXC), weights)).reshape(NTILE, TRACER_COUNT, NXC)
    flux_grid = jnp.zeros((NY, N_BLK, TRACER_COUNT, NXC), jnp.float32).at[grow, gcol].add(contrib)
    ocean_flux = jnp.transpose(flux_grid, (2, 0, 1, 3)).reshape(TRACER_COUNT, NY, NX)

    eastward_neighbour = 0.5 * (velocity[0] + jnp.roll(velocity[0], -1, axis=2))
    rowid = lax.broadcasted_iota(jnp.int32, (1, NY, 1), 1)
    boundary_wall = jnp.where(rowid == NY - 1, 0.0, 1.0).astype(jnp.float32)
    northward_neighbour = 0.5 * (velocity[1] + jnp.roll(velocity[1], -1, axis=1)) * boundary_wall
    efac = eastward_neighbour[:, None]
    nfac = northward_neighbour[:, None]
    forcing = FORCE * land[None] * ocean_flux

    ocean_state = tracer
    for step in range(NSTEP):
        flux_e = jnp.maximum(efac, 0.0) * ocean_state + jnp.minimum(efac, 0.0) * jnp.roll(ocean_state, -1, axis=3)
        flux_n = jnp.maximum(nfac, 0.0) * ocean_state + jnp.minimum(nfac, 0.0) * jnp.roll(ocean_state, -1, axis=2)
        tend = (jnp.roll(flux_e, 1, axis=3) - flux_e) + (jnp.roll(flux_n, 1, axis=2) - flux_n)
        star = ocean_state + wet[:, None] * tend
        star = star.at[0].add(forcing)
        ocean_state = column_solve(star, couple)

    top = jnp.transpose(ocean_state[0].reshape(TRACER_COUNT, NY, N_BLK, NXC), (1, 2, 0, 3))
    values = top[grow, gcol]

    def backward_map(item):
        rows_in, tiles = item
        return jnp.einsum("tfb,tab->tfa", rows_in, tiles.astype(jnp.float32), precision=HIGH)

    back = lax.map(backward_map, (values.reshape(DEVICES, KT, TRACER_COUNT, NXC), weights)).reshape(NTILE, TRACER_COUNT, NXC)
    atmosphere_return = jnp.zeros((DEVICES * ABLK, TRACER_COUNT, NXC), jnp.float32).at[gsrc].add(back)
    atmosphere_surface_tracer = jnp.transpose(atmosphere_return, (1, 0, 2)).reshape(TRACER_COUNT, ATMOS_COLUMNS)
    return ocean_state, atmosphere_surface_tracer
```

```python
import functools

import jax
import jax.numpy as jnp
from jax import lax
from jax.experimental import pallas as pl
from jax.experimental.pallas import tpu as pltpu
from jax.sharding import PartitionSpec as P

NSTEP = 4
FORCE = 0.25
HIGH = lax.Precision.HIGHEST
MESH = pl.DeviceIdType.MESH
UNROLL = 8


def ocean_kernel(
    n_blk, n_sub, tracer, velocity, kappa, kmt, land, flux, out,
    cc, cw, ce, cn, cs, md, gg, inv, col_out, row_out, col_in, row_in,
    col_send, row_send, col_recv, row_recv,
):
    levels, ntr, rows, cols = tracer.shape
    blk, sub = lax.axis_index("blk"), lax.axis_index("sub")
    east, west = lax.rem(blk + 1, n_blk), lax.rem(blk + n_blk - 1, n_blk)
    has_north, has_south = sub < n_sub - 1, sub > 0
    north, south = lax.rem(sub + 1, n_sub), lax.rem(sub + n_sub - 1, n_sub)
    lane = lax.broadcasted_iota(jnp.int32, (rows, cols), 1)
    row = lax.broadcasted_iota(jnp.int32, (rows, cols), 0)
    unroll = UNROLL if levels % UNROLL == 0 else 1
    zero = jnp.zeros((rows, cols), jnp.float32)

    barrier = pltpu.get_barrier_semaphore()
    pl.semaphore_signal(barrier, inc=1, device_id=(east, sub), device_id_type=MESH)
    pl.semaphore_signal(barrier, inc=1, device_id=(west, sub), device_id_type=MESH)

    @pl.when(has_north)
    def _():
        pl.semaphore_signal(barrier, inc=1, device_id=(blk, north), device_id_type=MESH)

    @pl.when(has_south)
    def _():
        pl.semaphore_signal(barrier, inc=1, device_id=(blk, south), device_id_type=MESH)

    pl.semaphore_wait(barrier, 2 + has_north.astype(jnp.int32) + has_south.astype(jnp.int32))

    def col_copy(step, side, count):
        return pltpu.make_async_remote_copy(
            src_ref=col_out.at[step, side, pl.ds(0, count)],
            dst_ref=col_in.at[step, side, pl.ds(0, count)],
            send_sem=col_send.at[step, side],
            recv_sem=col_recv.at[step, side],
            device_id=(east if side else west, sub),
            device_id_type=MESH,
        )

    def row_copy(step, side, count):
        return pltpu.make_async_remote_copy(
            src_ref=row_out.at[step, side, pl.ds(0, count)],
            dst_ref=row_in.at[step, side, pl.ds(0, count)],
            send_sem=row_send.at[step, side],
            recv_sem=row_recv.at[step, side],
            device_id=(blk, north if side else south),
            device_id_type=MESH,
        )

    def send(step, count):
        @pl.when(has_south)
        def _():
            row_copy(step, 0, count).start()

        @pl.when(has_north)
        def _():
            row_copy(step, 1, count).start()

        col_copy(step, 0, count).start()
        col_copy(step, 1, count).start()

    def receive(step, count):
        col_copy(step, 0, count).wait_recv()
        col_copy(step, 1, count).wait_recv()

        @pl.when(has_north)
        def _():
            row_copy(step, 0, count).wait_recv()

        @pl.when(has_south)
        def _():
            row_copy(step, 1, count).wait_recv()

    def finish(step, count):
        col_copy(step, 0, count).wait_send()
        col_copy(step, 1, count).wait_send()

        @pl.when(has_south)
        def _():
            row_copy(step, 0, count).wait_send()

        @pl.when(has_north)
        def _():
            row_copy(step, 1, count).wait_send()

    def loop(body, init, down=False):
        def group(i, carry):
            for j in range(unroll):
                k = i * unroll + j
                carry = body(levels - 1 - k if down else k, carry)
            return carry

        return lax.fori_loop(0, levels // unroll, group, init)

    def put_col(packed, value, k, side):
        shift = k if side == 0 else lax.rem(k + 1, cols)
        return jnp.where(lane == k, pltpu.roll(value, shift, 1), packed)

    def west_of(value, halo, k):
        return jnp.where(lane == 0, pltpu.roll(halo, lax.rem(cols - k, cols), 1), pltpu.roll(value, 1, 1))

    def east_of(value, halo, k):
        return jnp.where(lane == cols - 1, pltpu.roll(halo, cols - 1 - k, 1), pltpu.roll(value, cols - 1, 1))

    def north_of(value, halo):
        return jnp.where(row == rows - 1, halo, pltpu.roll(value, rows - 1, 0))

    def south_of(value, halo):
        return jnp.where(row == 0, halo, pltpu.roll(value, 1, 0))

    def pack_first(k, carry):
        carry = list(carry)
        for f in range(ntr + 1):
            value = tracer[k, f] if f < ntr else velocity[0, k]
            across = value if f < ntr else velocity[1, k]
            for side in range(2):
                carry[2 * f + side] = put_col(carry[2 * f + side], value, k, side)
            row_out[0, 0, f, pl.ds(k, 1), :] = across[:1]
            row_out[0, 1, f, pl.ds(k, 1), :] = across[rows - 1:]
        return tuple(carry)

    packed = loop(pack_first, (zero,) * (2 * ntr + 2))
    for f in range(ntr + 1):
        for side in range(2):
            col_out[0, side, f] = packed[2 * f + side]
    send(0, ntr + 1)

    @pl.when(jnp.logical_not(has_north))
    def _():
        row_in[:, 0] = jnp.zeros(row_in.shape[:1] + row_in.shape[2:], jnp.float32)

    @pl.when(jnp.logical_not(has_south))
    def _():
        row_in[:, 1] = jnp.zeros(row_in.shape[:1] + row_in.shape[2:], jnp.float32)

    wet_depth = jnp.where(land[...] > 0, kmt[...], 0)

    def factor(k, carry):
        below, hold = carry
        above = jnp.where(k < wet_depth, kappa[jnp.maximum(k - 1, 0)], 0.0)
        above = jnp.where(k > 0, above, 0.0)
        part = 1.0 + below * hold
        scale = 1.0 / (above + part)
        inv[k] = scale
        gg[k] = above * scale
        md[k] = below * scale
        return above, part * scale

    loop(factor, (zero, zero), down=True)
    receive(0, ntr + 1)

    wall_north = jnp.where((row == rows - 1) & jnp.logical_not(has_north), 0.0, 0.5)
    wall_south = jnp.where((row == 0) & jnp.logical_not(has_south), 0.0, 0.5)
    u_east, u_west = col_in[0, 0, ntr], col_in[0, 1, ntr]

    def stencil(k, carry):
        u, v = velocity[0, k], velocity[1, k]
        v_north = row_in[0, 0, ntr, pl.ds(k, 1), :]
        v_south = row_in[0, 1, ntr, pl.ds(k, 1), :]
        e = 0.5 * (u + east_of(u, u_east, k))
        w = 0.5 * (west_of(u, u_west, k) + u)
        n = wall_north * (v + north_of(v, v_north))
        s = wall_south * (south_of(v, v_south) + v)
        scale = inv[k]
        wet = jnp.where(k < wet_depth, scale, 0.0)
        cc[k] = scale + wet * (
            (jnp.minimum(w, 0.0) - jnp.maximum(e, 0.0)) + (jnp.minimum(s, 0.0) - jnp.maximum(n, 0.0))
        )
        cw[k] = wet * jnp.maximum(w, 0.0)
        ce[k] = -wet * jnp.minimum(e, 0.0)
        cs[k] = wet * jnp.maximum(s, 0.0)
        cn[k] = -wet * jnp.minimum(n, 0.0)
        return carry

    loop(stencil, 0)
    surface = jnp.where(land[...] > 0, FORCE, 0.0) * inv[0]

    for step in range(NSTEP):
        if step:
            receive(step, ntr)
        state = tracer if step == 0 else out
        halo_e = [col_in[step, 0, f] for f in range(ntr)]
        halo_w = [col_in[step, 1, f] for f in range(ntr)]

        def forward(k, carry):
            now = []
            for f in range(ntr):
                value = state[k, f]
                acc = cc[k] * value + md[k] * carry[f]
                acc += cw[k] * west_of(value, halo_w[f], k)
                acc += ce[k] * east_of(value, halo_e[f], k)
                acc += cn[k] * north_of(value, row_in[step, 0, f, pl.ds(k, 1), :])
                acc += cs[k] * south_of(value, row_in[step, 1, f, pl.ds(k, 1), :])
                out[k, f] = acc
                now.append(acc)
            return tuple(now)

        top = loop(forward, (zero,) * ntr, down=True)
        for f in range(ntr):
            out[0, f] = top[f] + surface * flux[f]

        last = step == NSTEP - 1

        def backward(k, carry):
            carry = list(carry)
            for f in range(ntr):
                value = out[k, f] + gg[k] * carry[f]
                out[k, f] = value
                carry[f] = value
                if not last:
                    for side in range(2):
                        at = ntr + 2 * f + side
                        carry[at] = put_col(carry[at], value, k, side)
                    row_out[step + 1, 0, f, pl.ds(k, 1), :] = value[:1]
                    row_out[step + 1, 1, f, pl.ds(k, 1), :] = value[rows - 1:]
            return tuple(carry)

        done = loop(backward, (zero,) * (ntr if last else 3 * ntr))
        if not last:
            for f in range(ntr):
                for side in range(2):
                    col_out[step + 1, side, f] = done[ntr + 2 * f + side]
            send(step + 1, ntr)

    for step in range(NSTEP):
        finish(step, ntr + 1 if step == 0 else ntr)


def ocean(n_blk, n_sub, tracer, velocity, kappa, kmt, land, flux):
    levels, ntr, rows, cols = tracer.shape
    field = pltpu.VMEM((levels, rows, cols), jnp.float32)
    vmem = pl.BlockSpec(memory_space=pltpu.VMEM)
    return pl.pallas_call(
        functools.partial(ocean_kernel, n_blk, n_sub),
        out_shape=jax.ShapeDtypeStruct(tracer.shape, jnp.float32),
        in_specs=[vmem] * 6,
        out_specs=vmem,
        scratch_shapes=[field] * 8
        + [
            pltpu.VMEM((NSTEP, 2, ntr + 1, rows, cols), jnp.float32),
            pltpu.VMEM((NSTEP, 2, ntr + 1, levels, cols), jnp.float32),
            pltpu.VMEM((NSTEP, 2, ntr + 1, rows, cols), jnp.float32),
            pltpu.VMEM((NSTEP, 2, ntr + 1, levels, cols), jnp.float32),
            pltpu.SemaphoreType.DMA((NSTEP, 2)),
            pltpu.SemaphoreType.DMA((NSTEP, 2)),
            pltpu.SemaphoreType.DMA((NSTEP, 2)),
            pltpu.SemaphoreType.DMA((NSTEP, 2)),
        ],
        compiler_params=pltpu.CompilerParams(
            collective_id=0, has_side_effects=True, vmem_limit_bytes=40 * 1024 * 1024
        ),
        name="ocean",
    )(tracer, velocity, kappa, kmt, land, flux)


def local(
    tracer, velocity, kappa, kmt, land_mask, atm_flux, remap_weight, remap_dest, remap_src_block, remap_dst_block
):
    levels, ntracer, rows, cols = tracer.shape
    n_blk = lax.axis_size("blk")
    n_sub = lax.axis_size("sub")
    devices = n_blk * n_sub
    tiles = remap_weight.shape[0]
    capacity = max(2, 2 * tiles // devices)
    slots = devices * capacity
    atm_blocks = atm_flux.shape[1] // cols
    weights32 = remap_weight.astype(jnp.float32)
    src_pick = (remap_src_block[:, None] == jnp.arange(atm_blocks, dtype=jnp.int32)[None]).astype(jnp.float32)
    atm_local = atm_flux.reshape(ntracer, atm_blocks, cols)
    blocks = jnp.einsum("tk,fkc->tfc", src_pick, atm_local, precision=HIGH)
    contrib = jnp.einsum("tfa,tab->tfb", blocks, weights32, precision=HIGH)
    dest = remap_dest[:, 0]
    same = (dest[:, None] == dest[None, :]) & (
        jnp.arange(tiles, dtype=jnp.int32)[:, None] > jnp.arange(tiles, dtype=jnp.int32)[None]
    )
    rank = jnp.sum(same.astype(jnp.int32), axis=1)
    slot_of = dest * capacity + rank
    place = (slot_of[:, None] == jnp.arange(slots, dtype=jnp.int32)[None]).astype(jnp.float32)
    named = jnp.broadcast_to(remap_dst_block.astype(jnp.float32)[:, None, None], (tiles, 1, cols))
    outgoing = jnp.einsum("ts,tfc->sfc", place, jnp.concatenate([contrib, named], axis=1), precision=HIGH)
    incoming = lax.all_to_all(
        outgoing.reshape(devices, capacity, ntracer + 1, cols),
        ("blk", "sub"),
        split_axis=0,
        concat_axis=0,
        tiled=True,
    ).reshape(slots, ntracer + 1, cols)
    got_rows = incoming[:, ntracer, 0].astype(jnp.int32)
    row_pick = (got_rows[:, None] == jnp.arange(rows, dtype=jnp.int32)[None]).astype(jnp.float32)
    ocean_flux = jnp.einsum("sr,sfc->frc", row_pick, incoming[:, :ntracer], precision=HIGH)
    ocean_state = ocean(n_blk, n_sub, tracer, velocity, kappa, kmt, land_mask, ocean_flux)
    surface_rows = jnp.einsum("sr,frc->sfc", row_pick, ocean_state[0], precision=HIGH)
    returned = lax.all_to_all(
        surface_rows.reshape(devices, capacity, ntracer, cols),
        ("blk", "sub"),
        split_axis=0,
        concat_axis=0,
        tiled=True,
    )
    returned = returned.reshape(slots, ntracer, cols)
    tile_values = jnp.einsum("ts,sfc->tfc", place, returned, precision=HIGH)
    back = jnp.einsum("tfb,tab->tfa", tile_values, weights32, precision=HIGH)
    atmosphere_return = jnp.einsum("tk,tfa->fka", src_pick, back, precision=HIGH)
    return (ocean_state, atmosphere_return.reshape(ntracer, atm_blocks * cols))


def solution(mesh):
    return jax.shard_map(
        local,
        mesh=mesh,
        in_specs=(
            P(None, None, "sub", "blk"),
            P(None, None, "sub", "blk"),
            P(None, "sub", "blk"),
            P("sub", "blk"),
            P("sub", "blk"),
            P(None, ("blk", "sub")),
            P(("blk", "sub"), None, None),
            P(("blk", "sub"), None),
            P(("blk", "sub")),
            P(("blk", "sub")),
        ),
        out_specs=(P(None, None, "sub", "blk"), P(None, ("blk", "sub"))),
        check_vma=False,
    )
```

```python
import functools

import jax
import jax.numpy as jnp
from jax import lax
from jax.experimental import pallas as pl
from jax.experimental.pallas import tpu as pltpu
from jax.sharding import PartitionSpec as P

NSTEP = 4
FORCE = 0.25
HIGH = lax.Precision.HIGHEST
MESH = pl.DeviceIdType.MESH
UNROLL = 8


def ocean_kernel(
    n_blk, n_sub, tracer, velocity, kappa, kmt, land, outgoing, out, returned,
    cc, cw, ce, cn, cs, md, gg, inv, col_out, row_out, col_in, row_in, inbox, back_out, back_in,
    col_send, row_send, col_recv, row_recv, flux_send, flux_recv, back_send, back_recv,
):
    levels, ntr, rows, cols = tracer.shape
    blk, sub = lax.axis_index("blk"), lax.axis_index("sub")
    east, west = lax.rem(blk + 1, n_blk), lax.rem(blk + n_blk - 1, n_blk)
    has_north, has_south = sub < n_sub - 1, sub > 0
    north, south = lax.rem(sub + 1, n_sub), lax.rem(sub + n_sub - 1, n_sub)
    lane = lax.broadcasted_iota(jnp.int32, (rows, cols), 1)
    row = lax.broadcasted_iota(jnp.int32, (rows, cols), 0)
    unroll = UNROLL if levels % UNROLL == 0 else 1
    zero = jnp.zeros((rows, cols), jnp.float32)

    barrier = pltpu.get_barrier_semaphore()
    devices, capacity = outgoing.shape[:2]
    me = blk * n_sub + sub

    def others(body):
        def one(i, carry):
            body(lax.rem(me + i, devices))
            return carry

        lax.fori_loop(1, devices, one, 0)

    def place_of(device):
        return (device // n_sub, lax.rem(device, n_sub))

    others(lambda d: pl.semaphore_signal(barrier, inc=1, device_id=place_of(d), device_id_type=MESH))
    pl.semaphore_wait(barrier, devices - 1)

    def flux_copy(source, target):
        return pltpu.make_async_remote_copy(
            src_ref=outgoing.at[target],
            dst_ref=inbox.at[source],
            send_sem=flux_send.at[target],
            recv_sem=flux_recv.at[source],
            device_id=place_of(target),
            device_id_type=MESH,
        )

    def back_copy(source, target):
        return pltpu.make_async_remote_copy(
            src_ref=back_out.at[target],
            dst_ref=back_in.at[source],
            send_sem=back_send.at[target],
            recv_sem=back_recv.at[source],
            device_id=place_of(target),
            device_id_type=MESH,
        )

    def col_copy(step, side, count):
        return pltpu.make_async_remote_copy(
            src_ref=col_out.at[step, side, pl.ds(0, count)],
            dst_ref=col_in.at[step, side, pl.ds(0, count)],
            send_sem=col_send.at[step, side],
            recv_sem=col_recv.at[step, side],
            device_id=(east if side else west, sub),
            device_id_type=MESH,
        )

    def row_copy(step, side, count):
        return pltpu.make_async_remote_copy(
            src_ref=row_out.at[step, side, pl.ds(0, count)],
            dst_ref=row_in.at[step, side, pl.ds(0, count)],
            send_sem=row_send.at[step, side],
            recv_sem=row_recv.at[step, side],
            device_id=(blk, north if side else south),
            device_id_type=MESH,
        )

    def send(step, count):
        @pl.when(has_south)
        def _():
            row_copy(step, 0, count).start()

        @pl.when(has_north)
        def _():
            row_copy(step, 1, count).start()

        col_copy(step, 0, count).start()
        col_copy(step, 1, count).start()

    def receive(step, count):
        col_copy(step, 0, count).wait_recv()
        col_copy(step, 1, count).wait_recv()

        @pl.when(has_north)
        def _():
            row_copy(step, 0, count).wait_recv()

        @pl.when(has_south)
        def _():
            row_copy(step, 1, count).wait_recv()

    def finish(step, count):
        col_copy(step, 0, count).wait_send()
        col_copy(step, 1, count).wait_send()

        @pl.when(has_south)
        def _():
            row_copy(step, 0, count).wait_send()

        @pl.when(has_north)
        def _():
            row_copy(step, 1, count).wait_send()

    def loop(body, init, down=False):
        def group(i, carry):
            for j in range(unroll):
                k = i * unroll + j
                carry = body(levels - 1 - k if down else k, carry)
            return carry

        return lax.fori_loop(0, levels // unroll, group, init)

    def put_col(packed, value, k, side):
        shift = k if side == 0 else lax.rem(k + 1, cols)
        return jnp.where(lane == k, pltpu.roll(value, shift, 1), packed)

    def west_of(value, halo, k):
        return jnp.where(lane == 0, pltpu.roll(halo, lax.rem(cols - k, cols), 1), pltpu.roll(value, 1, 1))

    def east_of(value, halo, k):
        return jnp.where(lane == cols - 1, pltpu.roll(halo, cols - 1 - k, 1), pltpu.roll(value, cols - 1, 1))

    def north_of(value, halo):
        return jnp.where(row == rows - 1, halo, pltpu.roll(value, rows - 1, 0))

    def south_of(value, halo):
        return jnp.where(row == 0, halo, pltpu.roll(value, 1, 0))

    def pack_first(k, carry):
        carry = list(carry)
        for f in range(ntr + 1):
            value = tracer[k, f] if f < ntr else velocity[0, k]
            across = value if f < ntr else velocity[1, k]
            for side in range(2):
                carry[2 * f + side] = put_col(carry[2 * f + side], value, k, side)
            row_out[0, 0, f, pl.ds(k, 1), :] = across[:1]
            row_out[0, 1, f, pl.ds(k, 1), :] = across[rows - 1:]
        return tuple(carry)

    packed = loop(pack_first, (zero,) * (2 * ntr + 2))
    for f in range(ntr + 1):
        for side in range(2):
            col_out[0, side, f] = packed[2 * f + side]
    send(0, ntr + 1)
    others(lambda d: flux_copy(me, d).start())
    inbox[me] = outgoing[me]

    @pl.when(jnp.logical_not(has_north))
    def _():
        row_in[:, 0] = jnp.zeros(row_in.shape[:1] + row_in.shape[2:], jnp.float32)

    @pl.when(jnp.logical_not(has_south))
    def _():
        row_in[:, 1] = jnp.zeros(row_in.shape[:1] + row_in.shape[2:], jnp.float32)

    wet_depth = jnp.where(land[...] > 0, kmt[...], 0)

    def factor(k, carry):
        below, hold = carry
        above = jnp.where(k < wet_depth, kappa[jnp.maximum(k - 1, 0)], 0.0)
        above = jnp.where(k > 0, above, 0.0)
        part = 1.0 + below * hold
        scale = 1.0 / (above + part)
        inv[k] = scale
        gg[k] = above * scale
        md[k] = below * scale
        return above, part * scale

    loop(factor, (zero, zero), down=True)
    receive(0, ntr + 1)

    wall_north = jnp.where((row == rows - 1) & jnp.logical_not(has_north), 0.0, 0.5)
    wall_south = jnp.where((row == 0) & jnp.logical_not(has_south), 0.0, 0.5)
    u_east, u_west = col_in[0, 0, ntr], col_in[0, 1, ntr]

    def stencil(k, carry):
        u, v = velocity[0, k], velocity[1, k]
        v_north = row_in[0, 0, ntr, pl.ds(k, 1), :]
        v_south = row_in[0, 1, ntr, pl.ds(k, 1), :]
        e = 0.5 * (u + east_of(u, u_east, k))
        w = 0.5 * (west_of(u, u_west, k) + u)
        n = wall_north * (v + north_of(v, v_north))
        s = wall_south * (south_of(v, v_south) + v)
        scale = inv[k]
        wet = jnp.where(k < wet_depth, scale, 0.0)
        cc[k] = scale + wet * (
            (jnp.minimum(w, 0.0) - jnp.maximum(e, 0.0)) + (jnp.minimum(s, 0.0) - jnp.maximum(n, 0.0))
        )
        cw[k] = wet * jnp.maximum(w, 0.0)
        ce[k] = -wet * jnp.minimum(e, 0.0)
        cs[k] = wet * jnp.maximum(s, 0.0)
        cn[k] = -wet * jnp.minimum(n, 0.0)
        return carry

    loop(stencil, 0)
    surface = jnp.where(land[...] > 0, FORCE, 0.0) * inv[0]

    def add_flux(device, totals):
        totals = list(totals)
        for c in range(capacity):
            message = inbox[device, pl.ds(c, 1), :]
            here = row == message[:, ntr * cols:].astype(jnp.int32)
            for f in range(ntr):
                totals[f] += jnp.where(here, message[:, f * cols:(f + 1) * cols], 0.0)
        return tuple(totals)

    def answer(device, top):
        for c in range(capacity):
            here = row == inbox[device, pl.ds(c, 1), pl.ds(ntr * cols, cols)].astype(jnp.int32)
            for f in range(ntr):
                back_out[device, pl.ds(c, 1), pl.ds(f * cols, cols)] = jnp.sum(
                    jnp.where(here, top[f], 0.0), axis=0, keepdims=True
                )

    for step in range(NSTEP):
        if step:
            receive(step, ntr)
        state = tracer if step == 0 else out
        halo_e = [col_in[step, 0, f] for f in range(ntr)]
        halo_w = [col_in[step, 1, f] for f in range(ntr)]

        def forward(k, carry):
            now = []
            for f in range(ntr):
                value = state[k, f]
                acc = cc[k] * value + md[k] * carry[f]
                acc += cw[k] * west_of(value, halo_w[f], k)
                acc += ce[k] * east_of(value, halo_e[f], k)
                acc += cn[k] * north_of(value, row_in[step, 0, f, pl.ds(k, 1), :])
                acc += cs[k] * south_of(value, row_in[step, 1, f, pl.ds(k, 1), :])
                out[k, f] = acc
                now.append(acc)
            return tuple(now)

        top = loop(forward, (zero,) * ntr, down=True)
        if step == 0:
            others(lambda d: flux_copy(d, me).wait_recv())
            flux = lax.fori_loop(0, devices, add_flux, (zero,) * ntr)
            flux = [surface * flux[f] for f in range(ntr)]
        top = [top[f] + flux[f] for f in range(ntr)]
        for f in range(ntr):
            out[0, f] = top[f]

        last = step == NSTEP - 1
        if last:
            def reply(d):
                answer(d, top)
                back_copy(me, d).start()

            others(reply)
            answer(me, top)

        def backward(k, carry):
            carry = list(carry)
            for f in range(ntr):
                value = out[k, f] + gg[k] * carry[f]
                out[k, f] = value
                carry[f] = value
                if not last:
                    for side in range(2):
                        at = ntr + 2 * f + side
                        carry[at] = put_col(carry[at], value, k, side)
                    row_out[step + 1, 0, f, pl.ds(k, 1), :] = value[:1]
                    row_out[step + 1, 1, f, pl.ds(k, 1), :] = value[rows - 1:]
            return tuple(carry)

        done = loop(backward, (zero,) * (ntr if last else 3 * ntr))
        if not last:
            for f in range(ntr):
                for side in range(2):
                    col_out[step + 1, side, f] = done[ntr + 2 * f + side]
            send(step + 1, ntr)

    for step in range(NSTEP):
        finish(step, ntr + 1 if step == 0 else ntr)
    returned[me] = back_out[me]

    def take(d):
        back_copy(d, me).wait_recv()
        returned[d] = back_in[d]

    others(take)
    others(lambda d: flux_copy(me, d).wait_send())
    others(lambda d: back_copy(me, d).wait_send())


def ocean(n_blk, n_sub, tracer, velocity, kappa, kmt, land, outgoing):
    levels, ntr, rows, cols = tracer.shape
    devices, capacity = outgoing.shape[:2]
    field = pltpu.VMEM((levels, rows, cols), jnp.float32)
    vmem = pl.BlockSpec(memory_space=pltpu.VMEM)
    return pl.pallas_call(
        functools.partial(ocean_kernel, n_blk, n_sub),
        out_shape=(
            jax.ShapeDtypeStruct(tracer.shape, jnp.float32),
            jax.ShapeDtypeStruct((devices, capacity, ntr * cols), jnp.float32),
        ),
        in_specs=[vmem] * 6,
        out_specs=(vmem, vmem),
        scratch_shapes=[field] * 8
        + [
            pltpu.VMEM((NSTEP, 2, ntr + 1, rows, cols), jnp.float32),
            pltpu.VMEM((NSTEP, 2, ntr + 1, levels, cols), jnp.float32),
            pltpu.VMEM((NSTEP, 2, ntr + 1, rows, cols), jnp.float32),
            pltpu.VMEM((NSTEP, 2, ntr + 1, levels, cols), jnp.float32),
            pltpu.VMEM(outgoing.shape, jnp.float32),
            pltpu.VMEM((devices, capacity, ntr * cols), jnp.float32),
            pltpu.VMEM((devices, capacity, ntr * cols), jnp.float32),
        ]
        + [pltpu.SemaphoreType.DMA((NSTEP, 2))] * 4
        + [pltpu.SemaphoreType.DMA((devices,))] * 4,
        compiler_params=pltpu.CompilerParams(
            collective_id=0, has_side_effects=True, vmem_limit_bytes=40 * 1024 * 1024
        ),
        name="ocean",
    )(tracer, velocity, kappa, kmt, land, outgoing)


def local(
    tracer, velocity, kappa, kmt, land_mask, atm_flux, remap_weight, remap_dest, remap_src_block, remap_dst_block
):
    levels, ntracer, rows, cols = tracer.shape
    n_blk = lax.axis_size("blk")
    n_sub = lax.axis_size("sub")
    devices = n_blk * n_sub
    tiles = remap_weight.shape[0]
    capacity = max(2, 2 * tiles // devices)
    slots = devices * capacity
    atm_blocks = atm_flux.shape[1] // cols
    weights32 = remap_weight.astype(jnp.float32)
    src_pick = (remap_src_block[:, None] == jnp.arange(atm_blocks, dtype=jnp.int32)[None]).astype(jnp.float32)
    atm_local = atm_flux.reshape(ntracer, atm_blocks, cols)
    blocks = jnp.einsum("tk,fkc->tfc", src_pick, atm_local, precision=HIGH)
    contrib = jnp.einsum("tfa,tab->tfb", blocks, weights32, precision=HIGH)
    dest = remap_dest[:, 0]
    same = (dest[:, None] == dest[None, :]) & (
        jnp.arange(tiles, dtype=jnp.int32)[:, None] > jnp.arange(tiles, dtype=jnp.int32)[None]
    )
    rank = jnp.sum(same.astype(jnp.int32), axis=1)
    slot_of = dest * capacity + rank
    place = (slot_of[:, None] == jnp.arange(slots, dtype=jnp.int32)[None]).astype(jnp.float32)
    named = jnp.broadcast_to(remap_dst_block.astype(jnp.float32)[:, None, None], (tiles, 1, cols))
    outgoing = jnp.einsum("ts,tfc->sfc", place, jnp.concatenate([contrib, named], axis=1), precision=HIGH)
    outgoing = outgoing.reshape(devices, capacity, (ntracer + 1) * cols)
    ocean_state, returned = ocean(n_blk, n_sub, tracer, velocity, kappa, kmt, land_mask, outgoing)
    returned = returned.reshape(slots, ntracer, cols)
    tile_values = jnp.einsum("ts,sfc->tfc", place, returned, precision=HIGH)
    back = jnp.einsum("tfb,tab->tfa", tile_values, weights32, precision=HIGH)
    atmosphere_return = jnp.einsum("tk,tfa->fka", src_pick, back, precision=HIGH)
    return (ocean_state, atmosphere_return.reshape(ntracer, atm_blocks * cols))


def solution(mesh):
    return jax.shard_map(
        local,
        mesh=mesh,
        in_specs=(
            P(None, None, "sub", "blk"),
            P(None, None, "sub", "blk"),
            P(None, "sub", "blk"),
            P("sub", "blk"),
            P("sub", "blk"),
            P(None, ("blk", "sub")),
            P(("blk", "sub"), None, None),
            P(("blk", "sub"), None),
            P(("blk", "sub")),
            P(("blk", "sub")),
        ),
        out_specs=(P(None, None, "sub", "blk"), P(None, ("blk", "sub"))),
        check_vma=False,
    )
```

```python
import functools

import jax
import jax.numpy as jnp
from jax import lax
from jax.experimental import pallas as pl
from jax.experimental.pallas import tpu as pltpu
from jax.sharding import PartitionSpec as P

NSTEP = 4
FORCE = 0.25
HIGH = lax.Precision.HIGHEST
MESH = pl.DeviceIdType.MESH
UNROLL = 16


def ocean_kernel(
    n_blk, n_sub, tracer, velocity, kappa, kmt, land, outgoing, out, returned,
    cc, cw, ce, cn, cs, md, gg, inv, col_out, row_out, col_in, row_in, inbox, back_out, back_in,
    col_send, row_send, col_recv, row_recv, flux_send, flux_recv, back_send, back_recv,
):
    levels, ntr, rows, cols = tracer.shape
    blk, sub = lax.axis_index("blk"), lax.axis_index("sub")
    east, west = lax.rem(blk + 1, n_blk), lax.rem(blk + n_blk - 1, n_blk)
    has_north, has_south = sub < n_sub - 1, sub > 0
    north, south = lax.rem(sub + 1, n_sub), lax.rem(sub + n_sub - 1, n_sub)
    lane = lax.broadcasted_iota(jnp.int32, (rows, cols), 1)
    row = lax.broadcasted_iota(jnp.int32, (rows, cols), 0)
    unroll = UNROLL if levels % UNROLL == 0 else 1
    zero = jnp.zeros((rows, cols), jnp.float32)

    barrier = pltpu.get_barrier_semaphore()
    devices, capacity = outgoing.shape[:2]
    me = blk * n_sub + sub

    def others(body):
        def one(i, carry):
            body(lax.rem(me + i, devices))
            return carry

        lax.fori_loop(1, devices, one, 0)

    def place_of(device):
        return (device // n_sub, lax.rem(device, n_sub))

    others(lambda d: pl.semaphore_signal(barrier, inc=1, device_id=place_of(d), device_id_type=MESH))
    pl.semaphore_wait(barrier, devices - 1)

    def flux_copy(source, target):
        return pltpu.make_async_remote_copy(
            src_ref=outgoing.at[target],
            dst_ref=inbox.at[source],
            send_sem=flux_send.at[target],
            recv_sem=flux_recv.at[source],
            device_id=place_of(target),
            device_id_type=MESH,
        )

    def back_copy(source, target):
        return pltpu.make_async_remote_copy(
            src_ref=back_out.at[target],
            dst_ref=back_in.at[source],
            send_sem=back_send.at[target],
            recv_sem=back_recv.at[source],
            device_id=place_of(target),
            device_id_type=MESH,
        )

    def col_copy(step, side, count):
        return pltpu.make_async_remote_copy(
            src_ref=col_out.at[step, side, pl.ds(0, count)],
            dst_ref=col_in.at[step, side, pl.ds(0, count)],
            send_sem=col_send.at[step, side],
            recv_sem=col_recv.at[step, side],
            device_id=(east if side else west, sub),
            device_id_type=MESH,
        )

    def row_copy(step, side, count):
        return pltpu.make_async_remote_copy(
            src_ref=row_out.at[step, side, pl.ds(0, count)],
            dst_ref=row_in.at[step, side, pl.ds(0, count)],
            send_sem=row_send.at[step, side],
            recv_sem=row_recv.at[step, side],
            device_id=(blk, north if side else south),
            device_id_type=MESH,
        )

    def send(step, count):
        @pl.when(has_south)
        def _():
            row_copy(step, 0, count).start()

        @pl.when(has_north)
        def _():
            row_copy(step, 1, count).start()

        col_copy(step, 0, count).start()
        col_copy(step, 1, count).start()

    def receive(step, count):
        col_copy(step, 0, count).wait_recv()
        col_copy(step, 1, count).wait_recv()

        @pl.when(has_north)
        def _():
            row_copy(step, 0, count).wait_recv()

        @pl.when(has_south)
        def _():
            row_copy(step, 1, count).wait_recv()

    def finish(step, count):
        col_copy(step, 0, count).wait_send()
        col_copy(step, 1, count).wait_send()

        @pl.when(has_south)
        def _():
            row_copy(step, 0, count).wait_send()

        @pl.when(has_north)
        def _():
            row_copy(step, 1, count).wait_send()

    def loop(body, init, down=False):
        def group(i, carry):
            for j in range(unroll):
                k = i * unroll + j
                carry = body(levels - 1 - k if down else k, carry)
            return carry

        return lax.fori_loop(0, levels // unroll, group, init)

    def put_col(packed, value, k, side):
        shift = k if side == 0 else lax.rem(k + 1, cols)
        return jnp.where(lane == k, pltpu.roll(value, shift, 1), packed)

    def west_of(value, halo, k):
        return jnp.where(lane == 0, pltpu.roll(halo, lax.rem(cols - k, cols), 1), pltpu.roll(value, 1, 1))

    def east_of(value, halo, k):
        return jnp.where(lane == cols - 1, pltpu.roll(halo, cols - 1 - k, 1), pltpu.roll(value, cols - 1, 1))

    def north_of(value, halo):
        return jnp.where(row == rows - 1, halo, pltpu.roll(value, rows - 1, 0))

    def south_of(value, halo):
        return jnp.where(row == 0, halo, pltpu.roll(value, 1, 0))

    def pack_first(k, carry):
        carry = list(carry)
        for f in range(ntr + 1):
            value = tracer[k, f] if f < ntr else velocity[0, k]
            across = value if f < ntr else velocity[1, k]
            for side in range(2):
                carry[2 * f + side] = put_col(carry[2 * f + side], value, k, side)
            row_out[0, 0, f, pl.ds(k, 1), :] = across[:1]
            row_out[0, 1, f, pl.ds(k, 1), :] = across[rows - 1:]
        return tuple(carry)

    packed = loop(pack_first, (zero,) * (2 * ntr + 2))
    for f in range(ntr + 1):
        for side in range(2):
            col_out[0, side, f] = packed[2 * f + side]
    send(0, ntr + 1)
    others(lambda d: flux_copy(me, d).start())
    inbox[me] = outgoing[me]

    @pl.when(jnp.logical_not(has_north))
    def _():
        row_in[:, 0] = jnp.zeros(row_in.shape[:1] + row_in.shape[2:], jnp.float32)

    @pl.when(jnp.logical_not(has_south))
    def _():
        row_in[:, 1] = jnp.zeros(row_in.shape[:1] + row_in.shape[2:], jnp.float32)

    wet_depth = jnp.where(land[...] > 0, kmt[...], 0)

    def factor(k, carry):
        below, hold = carry
        above = jnp.where(k < wet_depth, kappa[jnp.maximum(k - 1, 0)], 0.0)
        above = jnp.where(k > 0, above, 0.0)
        part = 1.0 + below * hold
        scale = 1.0 / (above + part)
        inv[k] = scale
        gg[k] = above * scale
        md[k] = below * scale
        return above, part * scale

    loop(factor, (zero, zero), down=True)
    receive(0, ntr + 1)

    wall_north = jnp.where((row == rows - 1) & jnp.logical_not(has_north), 0.0, 0.5)
    wall_south = jnp.where((row == 0) & jnp.logical_not(has_south), 0.0, 0.5)
    u_east, u_west = col_in[0, 0, ntr], col_in[0, 1, ntr]

    def stencil(k, carry):
        u, v = velocity[0, k], velocity[1, k]
        v_north = row_in[0, 0, ntr, pl.ds(k, 1), :]
        v_south = row_in[0, 1, ntr, pl.ds(k, 1), :]
        e = 0.5 * (u + east_of(u, u_east, k))
        w = 0.5 * (west_of(u, u_west, k) + u)
        n = wall_north * (v + north_of(v, v_north))
        s = wall_south * (south_of(v, v_south) + v)
        scale = inv[k]
        wet = jnp.where(k < wet_depth, scale, 0.0)
        cc[k] = scale + wet * (
            (jnp.minimum(w, 0.0) - jnp.maximum(e, 0.0)) + (jnp.minimum(s, 0.0) - jnp.maximum(n, 0.0))
        )
        cw[k] = wet * jnp.maximum(w, 0.0)
        ce[k] = -wet * jnp.minimum(e, 0.0)
        cs[k] = wet * jnp.maximum(s, 0.0)
        cn[k] = -wet * jnp.minimum(n, 0.0)
        return carry

    loop(stencil, 0)
    surface = jnp.where(land[...] > 0, FORCE, 0.0) * inv[0]

    def add_flux(device, totals):
        totals = list(totals)
        for c in range(capacity):
            message = inbox[device, pl.ds(c, 1), :]
            here = row == message[:, ntr * cols:].astype(jnp.int32)
            for f in range(ntr):
                totals[f] += jnp.where(here, message[:, f * cols:(f + 1) * cols], 0.0)
        return tuple(totals)

    def answer(device, top):
        for c in range(capacity):
            here = row == inbox[device, pl.ds(c, 1), pl.ds(ntr * cols, cols)].astype(jnp.int32)
            for f in range(ntr):
                back_out[device, pl.ds(c, 1), pl.ds(f * cols, cols)] = jnp.sum(
                    jnp.where(here, top[f], 0.0), axis=0, keepdims=True
                )

    for step in range(NSTEP):
        if step:
            receive(step, ntr)
        state = tracer if step == 0 else out
        halo_e = [col_in[step, 0, f] for f in range(ntr)]
        halo_w = [col_in[step, 1, f] for f in range(ntr)]

        def forward(i, carry):
            ks = [levels - 1 - (i * unroll + j) for j in range(unroll)]
            values = []
            for k in ks:
                for f in range(ntr):
                    value = state[k, f]
                    acc = cc[k] * value
                    acc += cw[k] * west_of(value, halo_w[f], k)
                    acc += ce[k] * east_of(value, halo_e[f], k)
                    acc += cn[k] * north_of(value, row_in[step, 0, f, pl.ds(k, 1), :])
                    acc += cs[k] * south_of(value, row_in[step, 1, f, pl.ds(k, 1), :])
                    values.append(acc)
            carry = list(carry)
            for j, k in enumerate(ks):
                for f in range(ntr):
                    carry[f] = values[j * ntr + f] + md[k] * carry[f]
                    values[j * ntr + f] = carry[f]
            for j, k in enumerate(ks):
                for f in range(ntr):
                    out[k, f] = values[j * ntr + f]
            return tuple(carry)

        top = lax.fori_loop(0, levels // unroll, forward, (zero,) * ntr)
        if step == 0:
            others(lambda d: flux_copy(d, me).wait_recv())
            flux = lax.fori_loop(0, devices, add_flux, (zero,) * ntr)
            flux = [surface * flux[f] for f in range(ntr)]
        top = [top[f] + flux[f] for f in range(ntr)]
        for f in range(ntr):
            out[0, f] = top[f]

        last = step == NSTEP - 1
        if last:
            def reply(d):
                answer(d, top)
                back_copy(me, d).start()

            others(reply)
            answer(me, top)

        def backward(i, carry):
            ks = [i * unroll + j for j in range(unroll)]
            carry = list(carry)
            values = [out[k, f] for k in ks for f in range(ntr)]
            for j, k in enumerate(ks):
                for f in range(ntr):
                    carry[f] = values[j * ntr + f] + gg[k] * carry[f]
                    values[j * ntr + f] = carry[f]
            for j, k in enumerate(ks):
                for f in range(ntr):
                    value = values[j * ntr + f]
                    out[k, f] = value
                    if not last:
                        for side in range(2):
                            at = ntr + 2 * f + side
                            carry[at] = put_col(carry[at], value, k, side)
                        row_out[step + 1, 0, f, pl.ds(k, 1), :] = value[:1]
                        row_out[step + 1, 1, f, pl.ds(k, 1), :] = value[rows - 1:]
            return tuple(carry)

        done = lax.fori_loop(0, levels // unroll, backward, (zero,) * (ntr if last else 3 * ntr))
        if not last:
            for f in range(ntr):
                for side in range(2):
                    col_out[step + 1, side, f] = done[ntr + 2 * f + side]
            send(step + 1, ntr)

    for step in range(NSTEP):
        finish(step, ntr + 1 if step == 0 else ntr)
    returned[me] = back_out[me]

    def take(d):
        back_copy(d, me).wait_recv()
        returned[d] = back_in[d]

    others(take)
    others(lambda d: flux_copy(me, d).wait_send())
    others(lambda d: back_copy(me, d).wait_send())


def ocean(n_blk, n_sub, tracer, velocity, kappa, kmt, land, outgoing):
    levels, ntr, rows, cols = tracer.shape
    devices, capacity = outgoing.shape[:2]
    field = pltpu.VMEM((levels, rows, cols), jnp.float32)
    vmem = pl.BlockSpec(memory_space=pltpu.VMEM)
    return pl.pallas_call(
        functools.partial(ocean_kernel, n_blk, n_sub),
        out_shape=(
            jax.ShapeDtypeStruct(tracer.shape, jnp.float32),
            jax.ShapeDtypeStruct((devices, capacity, ntr * cols), jnp.float32),
        ),
        in_specs=[vmem] * 6,
        out_specs=(vmem, vmem),
        scratch_shapes=[field] * 8
        + [
            pltpu.VMEM((NSTEP, 2, ntr + 1, rows, cols), jnp.float32),
            pltpu.VMEM((NSTEP, 2, ntr + 1, levels, cols), jnp.float32),
            pltpu.VMEM((NSTEP, 2, ntr + 1, rows, cols), jnp.float32),
            pltpu.VMEM((NSTEP, 2, ntr + 1, levels, cols), jnp.float32),
            pltpu.VMEM(outgoing.shape, jnp.float32),
            pltpu.VMEM((devices, capacity, ntr * cols), jnp.float32),
            pltpu.VMEM((devices, capacity, ntr * cols), jnp.float32),
        ]
        + [pltpu.SemaphoreType.DMA((NSTEP, 2))] * 4
        + [pltpu.SemaphoreType.DMA((devices,))] * 4,
        compiler_params=pltpu.CompilerParams(
            collective_id=0, has_side_effects=True, vmem_limit_bytes=40 * 1024 * 1024
        ),
        name="ocean",
    )(tracer, velocity, kappa, kmt, land, outgoing)


def local(
    tracer, velocity, kappa, kmt, land_mask, atm_flux, remap_weight, remap_dest, remap_src_block, remap_dst_block
):
    levels, ntracer, rows, cols = tracer.shape
    n_blk = lax.axis_size("blk")
    n_sub = lax.axis_size("sub")
    devices = n_blk * n_sub
    tiles = remap_weight.shape[0]
    capacity = max(2, 2 * tiles // devices)
    slots = devices * capacity
    atm_blocks = atm_flux.shape[1] // cols
    weights32 = remap_weight.astype(jnp.float32)
    src_pick = (remap_src_block[:, None] == jnp.arange(atm_blocks, dtype=jnp.int32)[None]).astype(jnp.float32)
    atm_local = atm_flux.reshape(ntracer, atm_blocks, cols)
    blocks = jnp.einsum("tk,fkc->tfc", src_pick, atm_local, precision=HIGH)
    contrib = jnp.einsum("tfa,tab->tfb", blocks, weights32, precision=HIGH)
    dest = remap_dest[:, 0]
    same = (dest[:, None] == dest[None, :]) & (
        jnp.arange(tiles, dtype=jnp.int32)[:, None] > jnp.arange(tiles, dtype=jnp.int32)[None]
    )
    rank = jnp.sum(same.astype(jnp.int32), axis=1)
    slot_of = dest * capacity + rank
    place = (slot_of[:, None] == jnp.arange(slots, dtype=jnp.int32)[None]).astype(jnp.float32)
    named = jnp.broadcast_to(remap_dst_block.astype(jnp.float32)[:, None, None], (tiles, 1, cols))
    outgoing = jnp.einsum("ts,tfc->sfc", place, jnp.concatenate([contrib, named], axis=1), precision=HIGH)
    outgoing = outgoing.reshape(devices, capacity, (ntracer + 1) * cols)
    ocean_state, returned = ocean(n_blk, n_sub, tracer, velocity, kappa, kmt, land_mask, outgoing)
    returned = returned.reshape(slots, ntracer, cols)
    tile_values = jnp.einsum("ts,sfc->tfc", place, returned, precision=HIGH)
    back = jnp.einsum("tfb,tab->tfa", tile_values, weights32, precision=HIGH)
    atmosphere_return = jnp.einsum("tk,tfa->fka", src_pick, back, precision=HIGH)
    return (ocean_state, atmosphere_return.reshape(ntracer, atm_blocks * cols))


def solution(mesh):
    return jax.shard_map(
        local,
        mesh=mesh,
        in_specs=(
            P(None, None, "sub", "blk"),
            P(None, None, "sub", "blk"),
            P(None, "sub", "blk"),
            P("sub", "blk"),
            P("sub", "blk"),
            P(None, ("blk", "sub")),
            P(("blk", "sub"), None, None),
            P(("blk", "sub"), None),
            P(("blk", "sub")),
            P(("blk", "sub")),
        ),
        out_specs=(P(None, None, "sub", "blk"), P(None, ("blk", "sub"))),
        check_vma=False,
    )
```

```python
import functools

import jax
import jax.numpy as jnp
from jax import lax
from jax.experimental import pallas as pl
from jax.experimental.pallas import tpu as pltpu
from jax.sharding import PartitionSpec as P

NSTEP = 4
FORCE = 0.25
HIGH = lax.Precision.HIGHEST
MESH = pl.DeviceIdType.MESH
UNROLL = 16


def ocean_kernel(
    n_blk, n_sub, tracer, velocity, kappa, kmt, land, outgoing, out, returned,
    cc, cw, ce, cn, cs, md, gg, inv, col_out, row_out, col_in, row_in, inbox, back_out, back_in,
    col_send, row_send, col_recv, row_recv, flux_send, flux_recv, back_send, back_recv,
):
    levels, ntr, rows, cols = tracer.shape
    blk, sub = lax.axis_index("blk"), lax.axis_index("sub")
    east, west = lax.rem(blk + 1, n_blk), lax.rem(blk + n_blk - 1, n_blk)
    has_north, has_south = sub < n_sub - 1, sub > 0
    north, south = lax.rem(sub + 1, n_sub), lax.rem(sub + n_sub - 1, n_sub)
    lane = lax.broadcasted_iota(jnp.int32, (rows, cols), 1)
    row = lax.broadcasted_iota(jnp.int32, (rows, cols), 0)
    unroll = UNROLL if levels % UNROLL == 0 else 1
    zero = jnp.zeros((rows, cols), jnp.float32)

    barrier = pltpu.get_barrier_semaphore()
    devices, capacity = outgoing.shape[:2]
    me = blk * n_sub + sub

    def others(body):
        def one(i, carry):
            body(lax.rem(me + i, devices))
            return carry

        lax.fori_loop(1, devices, one, 0)

    def place_of(device):
        return (device // n_sub, lax.rem(device, n_sub))

    others(lambda d: pl.semaphore_signal(barrier, inc=1, device_id=place_of(d), device_id_type=MESH))
    pl.semaphore_wait(barrier, devices - 1)

    def flux_copy(source, target):
        return pltpu.make_async_remote_copy(
            src_ref=outgoing.at[target],
            dst_ref=inbox.at[source],
            send_sem=flux_send,
            recv_sem=flux_recv,
            device_id=place_of(target),
            device_id_type=MESH,
        )

    def back_copy(source, target):
        return pltpu.make_async_remote_copy(
            src_ref=back_out.at[target],
            dst_ref=back_in.at[source],
            send_sem=back_send,
            recv_sem=back_recv,
            device_id=place_of(target),
            device_id_type=MESH,
        )

    def col_copy(step, side, count):
        return pltpu.make_async_remote_copy(
            src_ref=col_out.at[step, side, pl.ds(0, count)],
            dst_ref=col_in.at[step, side, pl.ds(0, count)],
            send_sem=col_send.at[step, side],
            recv_sem=col_recv.at[step, side],
            device_id=(east if side else west, sub),
            device_id_type=MESH,
        )

    def row_copy(step, side, count):
        return pltpu.make_async_remote_copy(
            src_ref=row_out.at[step, side, pl.ds(0, count)],
            dst_ref=row_in.at[step, side, pl.ds(0, count)],
            send_sem=row_send.at[step, side],
            recv_sem=row_recv.at[step, side],
            device_id=(blk, north if side else south),
            device_id_type=MESH,
        )

    def send(step, count):
        @pl.when(has_south)
        def _():
            row_copy(step, 0, count).start()

        @pl.when(has_north)
        def _():
            row_copy(step, 1, count).start()

        col_copy(step, 0, count).start()
        col_copy(step, 1, count).start()

    def receive(step, count):
        col_copy(step, 0, count).wait_recv()
        col_copy(step, 1, count).wait_recv()

        @pl.when(has_north)
        def _():
            row_copy(step, 0, count).wait_recv()

        @pl.when(has_south)
        def _():
            row_copy(step, 1, count).wait_recv()

    def finish(step, count):
        col_copy(step, 0, count).wait_send()
        col_copy(step, 1, count).wait_send()

        @pl.when(has_south)
        def _():
            row_copy(step, 0, count).wait_send()

        @pl.when(has_north)
        def _():
            row_copy(step, 1, count).wait_send()

    def loop(body, init, down=False):
        def group(i, carry):
            for j in range(unroll):
                k = i * unroll + j
                carry = body(levels - 1 - k if down else k, carry)
            return carry

        return lax.fori_loop(0, levels // unroll, group, init)

    def put_col(packed, value, k, side):
        shift = k if side == 0 else lax.rem(k + 1, cols)
        return jnp.where(lane == k, pltpu.roll(value, shift, 1), packed)

    def west_of(value, halo, k):
        return jnp.where(lane == 0, pltpu.roll(halo, lax.rem(cols - k, cols), 1), pltpu.roll(value, 1, 1))

    def east_of(value, halo, k):
        return jnp.where(lane == cols - 1, pltpu.roll(halo, cols - 1 - k, 1), pltpu.roll(value, cols - 1, 1))

    def north_of(value, halo):
        return jnp.where(row == rows - 1, halo, pltpu.roll(value, rows - 1, 0))

    def south_of(value, halo):
        return jnp.where(row == 0, halo, pltpu.roll(value, 1, 0))

    def pack_first(k, carry):
        carry = list(carry)
        for f in range(ntr + 1):
            value = tracer[k, f] if f < ntr else velocity[0, k]
            across = value if f < ntr else velocity[1, k]
            for side in range(2):
                carry[2 * f + side] = put_col(carry[2 * f + side], value, k, side)
            row_out[0, 0, f, pl.ds(k, 1), :] = across[:1]
            row_out[0, 1, f, pl.ds(k, 1), :] = across[rows - 1:]
        return tuple(carry)

    packed = loop(pack_first, (zero,) * (2 * ntr + 2))
    for f in range(ntr + 1):
        for side in range(2):
            col_out[0, side, f] = packed[2 * f + side]
    send(0, ntr + 1)
    others(lambda d: flux_copy(me, d).start())
    inbox[me] = outgoing[me]

    @pl.when(jnp.logical_not(has_north))
    def _():
        row_in[:, 0] = jnp.zeros(row_in.shape[:1] + row_in.shape[2:], jnp.float32)

    @pl.when(jnp.logical_not(has_south))
    def _():
        row_in[:, 1] = jnp.zeros(row_in.shape[:1] + row_in.shape[2:], jnp.float32)

    wet_depth = jnp.where(land[...] > 0, kmt[...], 0)

    def factor(k, carry):
        below, hold = carry
        above = jnp.where(k < wet_depth, kappa[jnp.maximum(k - 1, 0)], 0.0)
        above = jnp.where(k > 0, above, 0.0)
        part = 1.0 + below * hold
        scale = 1.0 / (above + part)
        inv[k] = scale
        gg[k] = above * scale
        md[k] = below * scale
        return above, part * scale

    loop(factor, (zero, zero), down=True)
    receive(0, ntr + 1)

    wall_north = jnp.where((row == rows - 1) & jnp.logical_not(has_north), 0.0, 0.5)
    wall_south = jnp.where((row == 0) & jnp.logical_not(has_south), 0.0, 0.5)
    u_east, u_west = col_in[0, 0, ntr], col_in[0, 1, ntr]

    def stencil(k, carry):
        u, v = velocity[0, k], velocity[1, k]
        v_north = row_in[0, 0, ntr, pl.ds(k, 1), :]
        v_south = row_in[0, 1, ntr, pl.ds(k, 1), :]
        e = 0.5 * (u + east_of(u, u_east, k))
        w = 0.5 * (west_of(u, u_west, k) + u)
        n = wall_north * (v + north_of(v, v_north))
        s = wall_south * (south_of(v, v_south) + v)
        scale = inv[k]
        wet = jnp.where(k < wet_depth, scale, 0.0)
        cc[k] = scale + wet * (
            (jnp.minimum(w, 0.0) - jnp.maximum(e, 0.0)) + (jnp.minimum(s, 0.0) - jnp.maximum(n, 0.0))
        )
        cw[k] = wet * jnp.maximum(w, 0.0)
        ce[k] = -wet * jnp.minimum(e, 0.0)
        cs[k] = wet * jnp.maximum(s, 0.0)
        cn[k] = -wet * jnp.minimum(n, 0.0)
        return carry

    loop(stencil, 0)
    surface = jnp.where(land[...] > 0, FORCE, 0.0) * inv[0]

    def all_of(out_ref, in_ref, send_sem, recv_sem):
        return pltpu.make_async_remote_copy(
            src_ref=out_ref.at[pl.ds(0, devices - 1)],
            dst_ref=in_ref.at[pl.ds(0, devices - 1)],
            send_sem=send_sem,
            recv_sem=recv_sem,
            device_id=(east, sub),
            device_id_type=MESH,
        )

    flux_all = all_of(outgoing, inbox, flux_send, flux_recv)
    back_all = all_of(back_out, back_in, back_send, back_recv)

    def grouped(body):
        def group(i, carry):
            for j in range(n_sub):
                carry = body(i * n_sub + j, carry)
            return carry

        return group

    def add_flux(device, totals):
        totals = list(totals)
        for c in range(capacity):
            message = inbox[device, pl.ds(c, 1), :]
            here = row == message[:, ntr * cols:].astype(jnp.int32)
            for f in range(ntr):
                totals[f] += jnp.where(here, message[:, f * cols:(f + 1) * cols], 0.0)
        return tuple(totals)

    def answer(device, top):
        for c in range(capacity):
            here = row == inbox[device, pl.ds(c, 1), pl.ds(ntr * cols, cols)].astype(jnp.int32)
            for f in range(ntr):
                back_out[device, pl.ds(c, 1), pl.ds(f * cols, cols)] = jnp.sum(
                    jnp.where(here, top[f], 0.0), axis=0, keepdims=True
                )
        return top

    for step in range(NSTEP):
        if step:
            receive(step, ntr)
        state = tracer if step == 0 else out
        halo_e = [col_in[step, 0, f] for f in range(ntr)]
        halo_w = [col_in[step, 1, f] for f in range(ntr)]

        def forward(i, carry):
            ks = [levels - 1 - (i * unroll + j) for j in range(unroll)]
            values = []
            for k in ks:
                for f in range(ntr):
                    value = state[k, f]
                    acc = cc[k] * value
                    acc += cw[k] * west_of(value, halo_w[f], k)
                    acc += ce[k] * east_of(value, halo_e[f], k)
                    acc += cn[k] * north_of(value, row_in[step, 0, f, pl.ds(k, 1), :])
                    acc += cs[k] * south_of(value, row_in[step, 1, f, pl.ds(k, 1), :])
                    values.append(acc)
            carry = list(carry)
            for j, k in enumerate(ks):
                for f in range(ntr):
                    carry[f] = values[j * ntr + f] + md[k] * carry[f]
                    values[j * ntr + f] = carry[f]
            for j, k in enumerate(ks):
                for f in range(ntr):
                    out[k, f] = values[j * ntr + f]
            return tuple(carry)

        top = lax.fori_loop(0, levels // unroll, forward, (zero,) * ntr)
        if step == 0:
            flux_all.wait_recv()
            flux = lax.fori_loop(0, n_blk, grouped(add_flux), (zero,) * ntr)
            flux = [surface * flux[f] for f in range(ntr)]
        top = [top[f] + flux[f] for f in range(ntr)]
        for f in range(ntr):
            out[0, f] = top[f]

        last = step == NSTEP - 1
        if last:
            lax.fori_loop(0, n_blk, grouped(answer), tuple(top))
            others(lambda d: back_copy(me, d).start())
            back_in[me] = back_out[me]

        def backward(i, carry):
            ks = [i * unroll + j for j in range(unroll)]
            carry = list(carry)
            values = [out[k, f] for k in ks for f in range(ntr)]
            for j, k in enumerate(ks):
                for f in range(ntr):
                    carry[f] = values[j * ntr + f] + gg[k] * carry[f]
                    values[j * ntr + f] = carry[f]
            for j, k in enumerate(ks):
                for f in range(ntr):
                    value = values[j * ntr + f]
                    out[k, f] = value
                    if not last:
                        for side in range(2):
                            at = ntr + 2 * f + side
                            carry[at] = put_col(carry[at], value, k, side)
                        row_out[step + 1, 0, f, pl.ds(k, 1), :] = value[:1]
                        row_out[step + 1, 1, f, pl.ds(k, 1), :] = value[rows - 1:]
            return tuple(carry)

        done = lax.fori_loop(0, levels // unroll, backward, (zero,) * (ntr if last else 3 * ntr))
        if not last:
            for f in range(ntr):
                for side in range(2):
                    col_out[step + 1, side, f] = done[ntr + 2 * f + side]
            send(step + 1, ntr)

    for step in range(NSTEP):
        finish(step, ntr + 1 if step == 0 else ntr)
    back_all.wait_recv()
    returned[...] = back_in[...]
    flux_all.wait_send()
    back_all.wait_send()


def ocean(n_blk, n_sub, tracer, velocity, kappa, kmt, land, outgoing):
    levels, ntr, rows, cols = tracer.shape
    devices, capacity = outgoing.shape[:2]
    field = pltpu.VMEM((levels, rows, cols), jnp.float32)
    vmem = pl.BlockSpec(memory_space=pltpu.VMEM)
    return pl.pallas_call(
        functools.partial(ocean_kernel, n_blk, n_sub),
        out_shape=(
            jax.ShapeDtypeStruct(tracer.shape, jnp.float32),
            jax.ShapeDtypeStruct((devices, capacity, ntr * cols), jnp.float32),
        ),
        in_specs=[vmem] * 6,
        out_specs=(vmem, vmem),
        scratch_shapes=[field] * 8
        + [
            pltpu.VMEM((NSTEP, 2, ntr + 1, rows, cols), jnp.float32),
            pltpu.VMEM((NSTEP, 2, ntr + 1, levels, cols), jnp.float32),
            pltpu.VMEM((NSTEP, 2, ntr + 1, rows, cols), jnp.float32),
            pltpu.VMEM((NSTEP, 2, ntr + 1, levels, cols), jnp.float32),
            pltpu.VMEM(outgoing.shape, jnp.float32),
            pltpu.VMEM((devices, capacity, ntr * cols), jnp.float32),
            pltpu.VMEM((devices, capacity, ntr * cols), jnp.float32),
        ]
        + [pltpu.SemaphoreType.DMA((NSTEP, 2))] * 4
        + [pltpu.SemaphoreType.DMA] * 4,
        compiler_params=pltpu.CompilerParams(
            collective_id=0, has_side_effects=True, vmem_limit_bytes=40 * 1024 * 1024
        ),
        name="ocean",
    )(tracer, velocity, kappa, kmt, land, outgoing)


def local(
    tracer, velocity, kappa, kmt, land_mask, atm_flux, remap_weight, remap_dest, remap_src_block, remap_dst_block
):
    levels, ntracer, rows, cols = tracer.shape
    n_blk = lax.axis_size("blk")
    n_sub = lax.axis_size("sub")
    devices = n_blk * n_sub
    tiles = remap_weight.shape[0]
    capacity = max(2, 2 * tiles // devices)
    slots = devices * capacity
    atm_blocks = atm_flux.shape[1] // cols
    weights32 = remap_weight.astype(jnp.float32)
    src_pick = (remap_src_block[:, None] == jnp.arange(atm_blocks, dtype=jnp.int32)[None]).astype(jnp.float32)
    atm_local = atm_flux.reshape(ntracer, atm_blocks, cols)
    blocks = jnp.einsum("tk,fkc->tfc", src_pick, atm_local, precision=HIGH)
    contrib = jnp.einsum("tfa,tab->tfb", blocks, weights32, precision=HIGH)
    dest = remap_dest[:, 0]
    same = (dest[:, None] == dest[None, :]) & (
        jnp.arange(tiles, dtype=jnp.int32)[:, None] > jnp.arange(tiles, dtype=jnp.int32)[None]
    )
    rank = jnp.sum(same.astype(jnp.int32), axis=1)
    slot_of = dest * capacity + rank
    place = (slot_of[:, None] == jnp.arange(slots, dtype=jnp.int32)[None]).astype(jnp.float32)
    named = jnp.broadcast_to(remap_dst_block.astype(jnp.float32)[:, None, None], (tiles, 1, cols))
    outgoing = jnp.einsum("ts,tfc->sfc", place, jnp.concatenate([contrib, named], axis=1), precision=HIGH)
    outgoing = outgoing.reshape(devices, capacity, (ntracer + 1) * cols)
    ocean_state, returned = ocean(n_blk, n_sub, tracer, velocity, kappa, kmt, land_mask, outgoing)
    returned = returned.reshape(slots, ntracer, cols)
    tile_values = jnp.einsum("ts,sfc->tfc", place, returned, precision=HIGH)
    back = jnp.einsum("tfb,tab->tfa", tile_values, weights32, precision=HIGH)
    atmosphere_return = jnp.einsum("tk,tfa->fka", src_pick, back, precision=HIGH)
    return (ocean_state, atmosphere_return.reshape(ntracer, atm_blocks * cols))


def solution(mesh):
    return jax.shard_map(
        local,
        mesh=mesh,
        in_specs=(
            P(None, None, "sub", "blk"),
            P(None, None, "sub", "blk"),
            P(None, "sub", "blk"),
            P("sub", "blk"),
            P("sub", "blk"),
            P(None, ("blk", "sub")),
            P(("blk", "sub"), None, None),
            P(("blk", "sub"), None),
            P(("blk", "sub")),
            P(("blk", "sub")),
        ),
        out_specs=(P(None, None, "sub", "blk"), P(None, ("blk", "sub"))),
        check_vma=False,
    )
```

```python
import functools

import jax
import jax.numpy as jnp
from jax import lax
from jax.experimental import pallas as pl
from jax.experimental.pallas import tpu as pltpu
from jax.sharding import PartitionSpec as P

NSTEP = 4
FORCE = 0.25
HIGH = lax.Precision.HIGH
MESH = pl.DeviceIdType.MESH
UNROLL = 16


def ocean_kernel(
    n_blk, n_sub, tracer, velocity, kappa, kmt, land, outgoing, out, returned,
    cc, cw, ce, cn, cs, md, gg, inv, col_out, row_out, col_in, row_in, inbox, back_out, back_in,
    col_send, row_send, col_recv, row_recv, flux_send, flux_recv, back_send, back_recv,
):
    levels, ntr, rows, cols = tracer.shape
    blk, sub = lax.axis_index("blk"), lax.axis_index("sub")
    east, west = lax.rem(blk + 1, n_blk), lax.rem(blk + n_blk - 1, n_blk)
    has_north, has_south = sub < n_sub - 1, sub > 0
    north, south = lax.rem(sub + 1, n_sub), lax.rem(sub + n_sub - 1, n_sub)
    lane = lax.broadcasted_iota(jnp.int32, (rows, cols), 1)
    row = lax.broadcasted_iota(jnp.int32, (rows, cols), 0)
    unroll = UNROLL if levels % UNROLL == 0 else 1
    zero = jnp.zeros((rows, cols), jnp.float32)

    barrier = pltpu.get_barrier_semaphore()
    devices, capacity = outgoing.shape[:2]
    me = blk * n_sub + sub

    def others(body):
        def one(i, carry):
            body(lax.rem(me + i, devices))
            return carry

        lax.fori_loop(1, devices, one, 0)

    def place_of(device):
        return (device // n_sub, lax.rem(device, n_sub))

    others(lambda d: pl.semaphore_signal(barrier, inc=1, device_id=place_of(d), device_id_type=MESH))
    pl.semaphore_wait(barrier, devices - 1)

    def flux_copy(source, target):
        return pltpu.make_async_remote_copy(
            src_ref=outgoing.at[target],
            dst_ref=inbox.at[source],
            send_sem=flux_send,
            recv_sem=flux_recv,
            device_id=place_of(target),
            device_id_type=MESH,
        )

    def back_copy(source, target):
        return pltpu.make_async_remote_copy(
            src_ref=back_out.at[target],
            dst_ref=back_in.at[source],
            send_sem=back_send,
            recv_sem=back_recv,
            device_id=place_of(target),
            device_id_type=MESH,
        )

    def col_copy(step, side, count):
        return pltpu.make_async_remote_copy(
            src_ref=col_out.at[step, side, pl.ds(0, count)],
            dst_ref=col_in.at[step, side, pl.ds(0, count)],
            send_sem=col_send.at[step, side],
            recv_sem=col_recv.at[step, side],
            device_id=(east if side else west, sub),
            device_id_type=MESH,
        )

    def row_copy(step, side, count):
        return pltpu.make_async_remote_copy(
            src_ref=row_out.at[step, side, pl.ds(0, count)],
            dst_ref=row_in.at[step, side, pl.ds(0, count)],
            send_sem=row_send.at[step, side],
            recv_sem=row_recv.at[step, side],
            device_id=(blk, north if side else south),
            device_id_type=MESH,
        )

    def send(step, count):
        @pl.when(has_south)
        def _():
            row_copy(step, 0, count).start()

        @pl.when(has_north)
        def _():
            row_copy(step, 1, count).start()

        col_copy(step, 0, count).start()
        col_copy(step, 1, count).start()

    def receive(step, count):
        col_copy(step, 0, count).wait_recv()
        col_copy(step, 1, count).wait_recv()

        @pl.when(has_north)
        def _():
            row_copy(step, 0, count).wait_recv()

        @pl.when(has_south)
        def _():
            row_copy(step, 1, count).wait_recv()

    def finish(step, count):
        col_copy(step, 0, count).wait_send()
        col_copy(step, 1, count).wait_send()

        @pl.when(has_south)
        def _():
            row_copy(step, 0, count).wait_send()

        @pl.when(has_north)
        def _():
            row_copy(step, 1, count).wait_send()

    def loop(body, init, down=False):
        def group(i, carry):
            for j in range(unroll):
                k = i * unroll + j
                carry = body(levels - 1 - k if down else k, carry)
            return carry

        return lax.fori_loop(0, levels // unroll, group, init)

    def put_col(packed, value, k, side):
        shift = k if side == 0 else lax.rem(k + 1, cols)
        return jnp.where(lane == k, pltpu.roll(value, shift, 1), packed)

    def west_of(value, halo, k):
        return jnp.where(lane == 0, pltpu.roll(halo, lax.rem(cols - k, cols), 1), pltpu.roll(value, 1, 1))

    def east_of(value, halo, k):
        return jnp.where(lane == cols - 1, pltpu.roll(halo, cols - 1 - k, 1), pltpu.roll(value, cols - 1, 1))

    def north_of(value, halo):
        return jnp.where(row == rows - 1, halo, pltpu.roll(value, rows - 1, 0))

    def south_of(value, halo):
        return jnp.where(row == 0, halo, pltpu.roll(value, 1, 0))

    def pack_first(k, carry):
        carry = list(carry)
        for f in range(ntr + 1):
            value = tracer[k, f] if f < ntr else velocity[0, k]
            across = value if f < ntr else velocity[1, k]
            for side in range(2):
                carry[2 * f + side] = put_col(carry[2 * f + side], value, k, side)
            row_out[0, 0, f, pl.ds(k, 1), :] = across[:1]
            row_out[0, 1, f, pl.ds(k, 1), :] = across[rows - 1:]
        return tuple(carry)

    packed = loop(pack_first, (zero,) * (2 * ntr + 2))
    for f in range(ntr + 1):
        for side in range(2):
            col_out[0, side, f] = packed[2 * f + side]
    send(0, ntr + 1)
    others(lambda d: flux_copy(me, d).start())
    inbox[me] = outgoing[me]

    @pl.when(jnp.logical_not(has_north))
    def _():
        row_in[:, 0] = jnp.zeros(row_in.shape[:1] + row_in.shape[2:], jnp.float32)

    @pl.when(jnp.logical_not(has_south))
    def _():
        row_in[:, 1] = jnp.zeros(row_in.shape[:1] + row_in.shape[2:], jnp.float32)

    wet_depth = jnp.where(land[...] > 0, kmt[...], 0)

    def factor(k, carry):
        below, hold = carry
        above = jnp.where(k < wet_depth, kappa[jnp.maximum(k - 1, 0)], 0.0)
        above = jnp.where(k > 0, above, 0.0)
        part = 1.0 + below * hold
        scale = 1.0 / (above + part)
        inv[k] = scale
        gg[k] = above * scale
        md[k] = below * scale
        return above, part * scale

    loop(factor, (zero, zero), down=True)
    receive(0, ntr + 1)

    wall_north = jnp.where((row == rows - 1) & jnp.logical_not(has_north), 0.0, 0.5)
    wall_south = jnp.where((row == 0) & jnp.logical_not(has_south), 0.0, 0.5)
    u_east, u_west = col_in[0, 0, ntr], col_in[0, 1, ntr]

    def stencil(k, carry):
        u, v = velocity[0, k], velocity[1, k]
        v_north = row_in[0, 0, ntr, pl.ds(k, 1), :]
        v_south = row_in[0, 1, ntr, pl.ds(k, 1), :]
        e = 0.5 * (u + east_of(u, u_east, k))
        w = 0.5 * (west_of(u, u_west, k) + u)
        n = wall_north * (v + north_of(v, v_north))
        s = wall_south * (south_of(v, v_south) + v)
        scale = inv[k]
        wet = jnp.where(k < wet_depth, scale, 0.0)
        cc[k] = scale + wet * (
            (jnp.minimum(w, 0.0) - jnp.maximum(e, 0.0)) + (jnp.minimum(s, 0.0) - jnp.maximum(n, 0.0))
        )
        cw[k] = wet * jnp.maximum(w, 0.0)
        ce[k] = -wet * jnp.minimum(e, 0.0)
        cs[k] = wet * jnp.maximum(s, 0.0)
        cn[k] = -wet * jnp.minimum(n, 0.0)
        return carry

    loop(stencil, 0)
    surface = jnp.where(land[...] > 0, FORCE, 0.0) * inv[0]

    def all_of(out_ref, in_ref, send_sem, recv_sem):
        return pltpu.make_async_remote_copy(
            src_ref=out_ref.at[pl.ds(0, devices - 1)],
            dst_ref=in_ref.at[pl.ds(0, devices - 1)],
            send_sem=send_sem,
            recv_sem=recv_sem,
            device_id=(east, sub),
            device_id_type=MESH,
        )

    flux_all = all_of(outgoing, inbox, flux_send, flux_recv)
    back_all = all_of(back_out, back_in, back_send, back_recv)

    def grouped(body):
        def group(i, carry):
            for j in range(n_sub):
                carry = body(i * n_sub + j, carry)
            return carry

        return group

    def add_flux(device, totals):
        totals = list(totals)
        for c in range(capacity):
            message = inbox[device, pl.ds(c, 1), :]
            here = row == message[:, ntr * cols:].astype(jnp.int32)
            for f in range(ntr):
                totals[f] += jnp.where(here, message[:, f * cols:(f + 1) * cols], 0.0)
        return tuple(totals)

    def answer(device, top):
        for c in range(capacity):
            here = row == inbox[device, pl.ds(c, 1), pl.ds(ntr * cols, cols)].astype(jnp.int32)
            for f in range(ntr):
                back_out[device, pl.ds(c, 1), pl.ds(f * cols, cols)] = jnp.sum(
                    jnp.where(here, top[f], 0.0), axis=0, keepdims=True
                )
        return top

    for step in range(NSTEP):
        if step:
            receive(step, ntr)
        state = tracer if step == 0 else out
        halo_e = [col_in[step, 0, f] for f in range(ntr)]
        halo_w = [col_in[step, 1, f] for f in range(ntr)]

        def forward(i, carry):
            ks = [levels - 1 - (i * unroll + j) for j in range(unroll)]
            values = []
            for k in ks:
                for f in range(ntr):
                    value = state[k, f]
                    acc = cc[k] * value
                    acc += cw[k] * west_of(value, halo_w[f], k)
                    acc += ce[k] * east_of(value, halo_e[f], k)
                    acc += cn[k] * north_of(value, row_in[step, 0, f, pl.ds(k, 1), :])
                    acc += cs[k] * south_of(value, row_in[step, 1, f, pl.ds(k, 1), :])
                    values.append(acc)
            carry = list(carry)
            for j, k in enumerate(ks):
                for f in range(ntr):
                    carry[f] = values[j * ntr + f] + md[k] * carry[f]
                    values[j * ntr + f] = carry[f]
            for j, k in enumerate(ks):
                for f in range(ntr):
                    out[k, f] = values[j * ntr + f]
            return tuple(carry)

        top = lax.fori_loop(0, levels // unroll, forward, (zero,) * ntr)
        if step == 0:
            flux_all.wait_recv()
            flux = lax.fori_loop(0, n_blk, grouped(add_flux), (zero,) * ntr)
            flux = [surface * flux[f] for f in range(ntr)]
        top = [top[f] + flux[f] for f in range(ntr)]
        for f in range(ntr):
            out[0, f] = top[f]

        last = step == NSTEP - 1
        if last:
            lax.fori_loop(0, n_blk, grouped(answer), tuple(top))
            others(lambda d: back_copy(me, d).start())
            back_in[me] = back_out[me]

        def backward(i, carry):
            ks = [i * unroll + j for j in range(unroll)]
            carry = list(carry)
            values = [out[k, f] for k in ks for f in range(ntr)]
            for j, k in enumerate(ks):
                for f in range(ntr):
                    carry[f] = values[j * ntr + f] + gg[k] * carry[f]
                    values[j * ntr + f] = carry[f]
            for j, k in enumerate(ks):
                for f in range(ntr):
                    value = values[j * ntr + f]
                    out[k, f] = value
                    if not last:
                        for side in range(2):
                            at = ntr + 2 * f + side
                            carry[at] = put_col(carry[at], value, k, side)
                        row_out[step + 1, 0, f, pl.ds(k, 1), :] = value[:1]
                        row_out[step + 1, 1, f, pl.ds(k, 1), :] = value[rows - 1:]
            return tuple(carry)

        done = lax.fori_loop(0, levels // unroll, backward, (zero,) * (ntr if last else 3 * ntr))
        if not last:
            for f in range(ntr):
                for side in range(2):
                    col_out[step + 1, side, f] = done[ntr + 2 * f + side]
            send(step + 1, ntr)

    for step in range(NSTEP):
        finish(step, ntr + 1 if step == 0 else ntr)
    back_all.wait_recv()
    returned[...] = back_in[...]
    flux_all.wait_send()
    back_all.wait_send()


def ocean(n_blk, n_sub, tracer, velocity, kappa, kmt, land, outgoing):
    levels, ntr, rows, cols = tracer.shape
    devices, capacity = outgoing.shape[:2]
    field = pltpu.VMEM((levels, rows, cols), jnp.float32)
    vmem = pl.BlockSpec(memory_space=pltpu.VMEM)
    return pl.pallas_call(
        functools.partial(ocean_kernel, n_blk, n_sub),
        out_shape=(
            jax.ShapeDtypeStruct(tracer.shape, jnp.float32),
            jax.ShapeDtypeStruct((devices, capacity, ntr * cols), jnp.float32),
        ),
        in_specs=[vmem] * 6,
        out_specs=(vmem, vmem),
        scratch_shapes=[field] * 8
        + [
            pltpu.VMEM((NSTEP, 2, ntr + 1, rows, cols), jnp.float32),
            pltpu.VMEM((NSTEP, 2, ntr + 1, levels, cols), jnp.float32),
            pltpu.VMEM((NSTEP, 2, ntr + 1, rows, cols), jnp.float32),
            pltpu.VMEM((NSTEP, 2, ntr + 1, levels, cols), jnp.float32),
            pltpu.VMEM(outgoing.shape, jnp.float32),
            pltpu.VMEM((devices, capacity, ntr * cols), jnp.float32),
            pltpu.VMEM((devices, capacity, ntr * cols), jnp.float32),
        ]
        + [pltpu.SemaphoreType.DMA((NSTEP, 2))] * 4
        + [pltpu.SemaphoreType.DMA] * 4,
        compiler_params=pltpu.CompilerParams(
            collective_id=0, has_side_effects=True, vmem_limit_bytes=40 * 1024 * 1024
        ),
        name="ocean",
    )(tracer, velocity, kappa, kmt, land, outgoing)


def local(
    tracer, velocity, kappa, kmt, land_mask, atm_flux, remap_weight, remap_dest, remap_src_block, remap_dst_block
):
    levels, ntracer, rows, cols = tracer.shape
    n_blk = lax.axis_size("blk")
    n_sub = lax.axis_size("sub")
    devices = n_blk * n_sub
    tiles = remap_weight.shape[0]
    capacity = max(2, 2 * tiles // devices)
    slots = devices * capacity
    atm_blocks = atm_flux.shape[1] // cols
    weights32 = remap_weight.astype(jnp.float32)
    src_pick = (remap_src_block[:, None] == jnp.arange(atm_blocks, dtype=jnp.int32)[None]).astype(jnp.float32)
    atm_local = atm_flux.reshape(ntracer, atm_blocks, cols)
    blocks = jnp.einsum("tk,fkc->tfc", src_pick, atm_local, precision=HIGH)
    contrib = jnp.einsum("tfa,tab->tfb", blocks, weights32, precision=HIGH)
    dest = remap_dest[:, 0]
    same = (dest[:, None] == dest[None, :]) & (
        jnp.arange(tiles, dtype=jnp.int32)[:, None] > jnp.arange(tiles, dtype=jnp.int32)[None]
    )
    rank = jnp.sum(same.astype(jnp.int32), axis=1)
    slot_of = dest * capacity + rank
    place = (slot_of[:, None] == jnp.arange(slots, dtype=jnp.int32)[None]).astype(jnp.float32)
    named = jnp.broadcast_to(remap_dst_block.astype(jnp.float32)[:, None, None], (tiles, 1, cols))
    outgoing = jnp.einsum("ts,tfc->sfc", place, jnp.concatenate([contrib, named], axis=1), precision=HIGH)
    outgoing = outgoing.reshape(devices, capacity, (ntracer + 1) * cols)
    ocean_state, returned = ocean(n_blk, n_sub, tracer, velocity, kappa, kmt, land_mask, outgoing)
    returned = returned.reshape(slots, ntracer, cols)
    tile_values = jnp.einsum("ts,sfc->tfc", place, returned, precision=HIGH)
    back = jnp.einsum("tfb,tab->tfa", tile_values, weights32, precision=HIGH)
    atmosphere_return = jnp.einsum("tk,tfa->fka", src_pick, back, precision=HIGH)
    return (ocean_state, atmosphere_return.reshape(ntracer, atm_blocks * cols))


def solution(mesh):
    return jax.shard_map(
        local,
        mesh=mesh,
        in_specs=(
            P(None, None, "sub", "blk"),
            P(None, None, "sub", "blk"),
            P(None, "sub", "blk"),
            P("sub", "blk"),
            P("sub", "blk"),
            P(None, ("blk", "sub")),
            P(("blk", "sub"), None, None),
            P(("blk", "sub"), None),
            P(("blk", "sub")),
            P(("blk", "sub")),
        ),
        out_specs=(P(None, None, "sub", "blk"), P(None, ("blk", "sub"))),
        check_vma=False,
    )
```
